256 devices in a mesh: row: 16 (over x_lo, z), col: 16 (over x_hi, y, core).
Axes of the slice: x: 4 (x_hi: 2, x_lo: 2; x = x_hi * 2 + x_lo), y: 4, z: 8, core: 2. Of those that a mesh axis runs over, the one named last changes fastest.
Arguments:
- counts: int32 [16], replicated, may hold values from 32 to 128, as said below
- cotangent: bfloat16 [2048, 16384], P('col', 'row'), may hold values from -1.1953125 to 1.1953125
- saved_gate: bfloat16 [2048, 26624], P('row', 'col'), may hold values from -9 to 9
- saved_up: bfloat16 [2048, 26624], P('row', 'col'), may hold values from -6 to 6
- down_weight: bfloat16 [26624, 16384], P('col', 'row'), may hold values from -0.0390625 to 0.0390625
Outputs:
- grad_gate: bfloat16 [2048, 26624], P('row', 'col')
- grad_up: bfloat16 [2048, 26624], P('row', 'col')
- grad_down: bfloat16 [26624, 16384], P('col', 'row')
The draws below stay inside these ranges and needn't reach their ends.
Inputs may be any that keep to these rules, and one draw needn't show every extreme that they name: `counts`: each count is a multiple of 32; in every draw some group has 128 live tokens and another only 32.
All inputs are finite; a program needn't handle non-finite values.
Results may differ from the reference program's by a relative error of at most 0.0049.
Values may be sent and summed in bfloat16 or wider, within the bound.
A program may use at most 128 MiB of HBM per device.

```python
import jax
import jax.numpy as jnp

D = 16384
FF = 26624
BLOCK = 32
TOK_DEV = 128
TOKENS = 2048
N_ROW = 16


def draw_counts(key, part):
    key = jax.random.fold_in(key, 7)
    first, second = jax.random.split(key, 2)
    most_blocks = TOK_DEV // BLOCK
    blocks = jax.random.randint(first, (N_ROW,), 1, most_blocks + 1)
    order = jax.random.permutation(second, N_ROW)
    blocks = jnp.where(order == 0, most_blocks, jnp.where(order == 1, 1, blocks))
    return (blocks * BLOCK).astype(jnp.int32)


def shard_levels(stream_key, shape, shards, smallest, largest):
    loudness, own = 1.0, jax.random.fold_in(stream_key, 6)
    for position, shards_of in shards:
        draws = jnp.exp(jax.random.uniform(jax.random.fold_in(own, position), (shards_of,), jnp.float32, smallest / len(shards), largest / len(shards)))
        loudness = loudness * jnp.repeat(draws, shape[position] // shards_of).reshape([-1 if axis == position else 1 for axis in range(len(shape))])
    return loudness


def centred(stream_key, dims, width, reach, cuts=(), kind=jnp.bfloat16):
    drawn = width * jax.random.normal(stream_key, dims, jnp.float32)
    if cuts:
        drawn = drawn * shard_levels(stream_key, dims, cuts, -0.22, 0.18)
    return jnp.clip(drawn, -reach, reach).astype(kind)


def setup_inputs(seed: int = 0) -> dict:
    seeds = jax.random.split(jax.random.key(seed), 6)
    counts = draw_counts(jax.random.fold_in(seeds[5], 71), 0)
    cotangent = centred(seeds[1], (TOKENS, D), 0.2, 1.1953125, ((0, 16), (1, 16)))
    saved_gate = centred(seeds[2], (TOKENS, FF), 1.5, 9.0, ((0, 16), (1, 16)))
    saved_up = centred(seeds[3], (TOKENS, FF), 1.0, 6.0, ((0, 16), (1, 16)))
    down_weight = centred(seeds[4], (FF, D), FF ** -0.5, 0.0390625, ((0, 16), (1, 16)))
    return dict(counts=counts, cotangent=cotangent, saved_gate=saved_gate, saved_up=saved_up, down_weight=down_weight)


def reference(counts, cotangent, saved_gate, saved_up, down_weight):
    index = jnp.arange(TOKENS, dtype=jnp.int32)
    live = (index % TOK_DEV) < counts[index // TOK_DEV]
    grad_out = jnp.where(live[:, None], cotangent, jnp.zeros_like(cotangent))
    grad_hidden = jnp.dot(grad_out, down_weight.T, preferred_element_type=jnp.float32)
    gate_float = saved_gate.astype(jnp.float32)
    up_float = saved_up.astype(jnp.float32)
    sigmoid_gate = jax.nn.sigmoid(gate_float)
    silu_gate = gate_float * sigmoid_gate
    hidden = (silu_gate * up_float).astype(jnp.bfloat16)
    grad_up = (grad_hidden * silu_gate).astype(jnp.bfloat16)
    slope = sigmoid_gate * (1.0 + gate_float * (1.0 - sigmoid_gate))
    grad_gate = (grad_hidden * up_float * slope).astype(jnp.bfloat16)
    grad_down = jnp.dot(hidden.T, grad_out, preferred_element_type=jnp.float32).astype(jnp.bfloat16)
    return grad_gate, grad_up, grad_down
```

```python
import jax
import jax.numpy as jnp
from jax import lax
from jax.experimental import pallas as pl
from jax.experimental.pallas import tpu as pltpu
from jax.sharding import PartitionSpec as P

MESH = pl.DeviceIdType.MESH
GROUPS = 16
TOK = 128
LANES = 128
HOPS = 8
CYCLES = (
    ("zig", 0, 0, 4),
    ("zig", 1, 4, 4),
    ("loop", 0, 8, 1),
    ("loop", 1, 9, 1),
    ("loop", 3, 10, 1),
    ("loop", 4, 11, 1),
    ("loop", 6, 12, 1),
)
TILES = 13
SOURCES = ((0, 0), (1, 0), (0, 1), (0, 3), (0, 2), (1, 1), (1, 3), (1, 2))


def place(cycle, p):
    kind, cut = cycle[:2]
    p = lax.rem(p + 2 * GROUPS, GROUPS)
    if kind == "zig":
        z = p // 2
        x = lax.rem(p + z + cut, 2)
        return x * 8 + z
    x = p // 8
    z = x * (15 - p) + (1 - x) * p
    return x * 8 + lax.rem(z + cut + 1, 8)


def spot(cycle, row):
    kind, cut = cycle[:2]
    x = row // 8
    z = lax.rem(row, 8)
    if kind == "zig":
        return 2 * z + lax.rem(x + z + cut, 2)
    z = lax.rem(z + 15 - cut, 8)
    return x * (15 - z) + (1 - x) * z


def hops_of(i, d):
    return HOPS if (i + d) % 2 == 0 else HOPS - 1


def kernel(
    counts_ref, cot_ref, gate_ref, up_ref, weight_hbm,
    grad_gate_ref, grad_up_ref, grad_down_ref,
    weight, cot, hid, part, stage, arrived,
    weight_sem, cot_send, cot_recv, core_send, core_recv,
    hid_send, hid_recv, sum_send, sum_recv,
):
    row = lax.axis_index("row")
    col = lax.axis_index("col")
    x, z = row // 8, lax.rem(row, 8)
    xh = col // 8
    y = lax.rem(col // 2, 4)
    core = lax.rem(col, 2)

    def at_col(dx, dy, c):
        return lax.rem(xh + dx, 2) * 8 + lax.rem(y + dy, 4) * 2 + c

    load_weight = pltpu.make_async_copy(weight_hbm, weight, weight_sem)
    load_weight.start()

    barrier = pltpu.get_barrier_semaphore()
    rows = [(1 - x) * 8 + z, x * 8 + lax.rem(z + 1, 8), x * 8 + lax.rem(z + 7, 8)]
    cols = [at_col(0, 0, 1 - core)] + [at_col(dx, dy, core) for dx, dy in SOURCES[1:5]]
    for other in rows:
        pl.semaphore_signal(barrier, inc=1, device_id={"row": other}, device_id_type=MESH)
    for other in cols:
        pl.semaphore_signal(barrier, inc=1, device_id={"col": other}, device_id_type=MESH)

    limit = counts_ref[col]
    token = lax.broadcasted_iota(jnp.int32, cot_ref.shape, 0)
    cot[col] = jnp.where(token < limit, cot_ref[...], jnp.zeros_like(cot_ref))
    for t in range(TILES):
        lanes = pl.ds(t * LANES, LANES)
        g = gate_ref[:, lanes].astype(jnp.float32)
        u = up_ref[:, lanes].astype(jnp.float32)
        hid[row, lanes, :] = (g * jax.nn.sigmoid(g) * u).T.astype(jnp.bfloat16)
    pl.semaphore_wait(barrier, len(rows) + len(cols))

    def cot_copy(q):
        dx, dy = SOURCES[q]
        block = cot.at[at_col(dx if dy else 0, 0, core)]
        target = at_col(0, 4 - dy, core) if dy else at_col(1, 0, core)
        return pltpu.make_async_remote_copy(
            src_ref=block, dst_ref=block, send_sem=cot_send.at[q], recv_sem=cot_recv.at[q],
            device_id={"col": target}, device_id_type=MESH,
        )

    def source(q):
        dx = jnp.where((q == 1) | (q > 4), 1, 0)
        dy = jnp.where((q == 2) | (q == 5), 1, 0) + jnp.where((q == 3) | (q == 6), 3, 0)
        dy = dy + jnp.where((q == 4) | (q == 7), 2, 0)
        return dx, dy

    def core_copy(q):
        dx, dy = source(q)
        block = cot.at[at_col(dx, dy, core)]
        return pltpu.make_async_remote_copy(
            src_ref=block, dst_ref=block, send_sem=core_send.at[q], recv_sem=core_recv.at[q],
            device_id={"col": at_col(0, 0, 1 - core)}, device_id_type=MESH,
        )

    def core_arrival(q):
        dx, dy = source(q)
        block = cot.at[at_col(dx, dy, 1 - core)]
        return pltpu.make_async_remote_copy(
            src_ref=block, dst_ref=block, send_sem=core_send.at[q], recv_sem=core_recv.at[q],
            device_id={"col": at_col(0, 0, 1 - core)}, device_id_type=MESH,
        )

    def cot_arrival(q):
        dx, dy = source(q)
        block = cot.at[at_col(dx, dy, core)]
        return pltpu.make_async_remote_copy(
            src_ref=block, dst_ref=block, send_sem=cot_send.at[q], recv_sem=cot_recv.at[q],
            device_id={"col": at_col(0, 0, 1 - core)}, device_id_type=MESH,
        )

    def hid_copy(i, d, s, shift=0):
        cycle = CYCLES[i]
        p = spot(cycle, row)
        way = 1 - 2 * d
        block = hid.at[
            place(cycle, p - way * (s + shift)),
            pl.ds(cycle[2] * LANES, cycle[3] * LANES),
        ]
        return pltpu.make_async_remote_copy(
            src_ref=block, dst_ref=block, send_sem=hid_send.at[i, d, s], recv_sem=hid_recv.at[i, d, s],
            device_id={"row": place(cycle, p + way)}, device_id_type=MESH,
        )

    def sum_copy(i, d, s):
        cycle = CYCLES[i]
        tiles = pl.ds(cycle[2], cycle[3])
        return pltpu.make_async_remote_copy(
            src_ref=stage.at[d, s, tiles], dst_ref=arrived.at[d, s, tiles],
            send_sem=sum_send.at[i, d, s], recv_sem=sum_recv.at[i, d, s],
            device_id={"row": place(cycle, spot(cycle, row) + 1 - 2 * d)}, device_id_type=MESH,
        )

    def each(s, run):
        for i in range(len(CYCLES)):
            for d in range(2):
                if hops_of(i, d) < HOPS:
                    pl.when(s < HOPS - 1)(lambda i=i, d=d: run(i, d))
                else:
                    run(i, d)

    for q in range(1, 5):
        cot_copy(q).start()
    core_copy(0).start()

    def gather_step(s, carry):
        @pl.when(s < HOPS)
        def _():
            def run(i, d):
                @pl.when(s > 0)
                def _():
                    hid_copy(i, d, s - 1, 1).wait_recv()

                hid_copy(i, d, s).start()

            each(s, run)

        @pl.when((s > 0) & (s < HOPS))
        def _():
            cot_arrival(s).wait_recv()
            core_copy(s).start()

        @pl.when(s == 1)
        def _():
            for q in range(5, 8):
                cot_copy(q).start()
            load_weight.wait()

        @pl.when(s > 0)
        def _():
            core_arrival(s - 1).wait_recv()
            dx, dy = source(s - 1)
            first = at_col(dx, dy, 0)
            block = cot[pl.ds(first, 2)].reshape(2 * TOK, cot.shape[2])
            for t in range(0, TILES, 2):
                n = min(2, TILES - t)
                product = lax.dot_general(
                    block, weight[t * LANES:(t + n) * LANES, :], (((1,), (1,)), ((), ())),
                    preferred_element_type=jnp.float32,
                )
                for k in range(n):
                    piece = product[:, k * LANES:(k + 1) * LANES]
                    part[pl.ds(first, 2), t + k] = piece.reshape(2, TOK, LANES)

        return carry

    lax.fori_loop(0, HOPS + 1, gather_step, 0)

    def sum_send_step(s, received):
        def run(i, d):
            cycle = CYCLES[i]
            tiles = pl.ds(cycle[2], cycle[3])
            owner = place(cycle, spot(cycle, row) + (1 - 2 * d) * (hops_of(i, d) - s))
            value = part[owner, tiles]
            if received:
                sum_copy(i, d, s - 1).wait_recv()
                value = value + arrived[d, s - 1, tiles].astype(jnp.float32)
            stage[d, s, tiles] = value.astype(jnp.bfloat16)
            sum_copy(i, d, s).start()

        each(s, run)

    sum_send_step(0, False)
    for i in range(len(CYCLES)):
        for d in range(2):
            hid_copy(i, d, hops_of(i, d) - 1, 1).wait_recv()

    def down(first, n):
        lhs = jnp.concatenate([hid[g, pl.ds(first, n), :] for g in range(GROUPS)], axis=1)
        grad_down_ref[pl.ds(first, n), :] = jnp.dot(
            lhs, cot[...].reshape(GROUPS * TOK, cot.shape[2]), preferred_element_type=jnp.float32
        ).astype(jnp.bfloat16)

    def sum_step(s, carry):
        sum_send_step(s, True)

        @pl.when(s < HOPS - 1)
        def _():
            down(pl.multiple_of((s - 1) * 2 * LANES, 2 * LANES), 2 * LANES)

        return carry

    lax.fori_loop(1, HOPS, sum_step, 0)
    down((TILES - 1) * LANES, LANES)

    for i, (kind, cut, first, count) in enumerate(CYCLES):
        for d in range(2):
            sum_copy(i, d, hops_of(i, d) - 1).wait_recv()
        for t in range(first, first + count):
            lanes = pl.ds(t * LANES, LANES)
            grad = part[row, t]
            for d in range(2):
                grad = grad + arrived[d, hops_of(i, d) - 1, t].astype(jnp.float32)
            g = gate_ref[:, lanes].astype(jnp.float32)
            u = up_ref[:, lanes].astype(jnp.float32)
            sig = jax.nn.sigmoid(g)
            grad_up_ref[:, lanes] = (grad * (g * sig)).astype(jnp.bfloat16)
            slope = sig * (1.0 + g * (1.0 - sig))
            grad_gate_ref[:, lanes] = (grad * u * slope).astype(jnp.bfloat16)

    def drain(s, carry):
        def run(i, d):
            hid_copy(i, d, s).wait_send()
            sum_copy(i, d, s).wait_send()

        each(s, run)
        core_copy(s).wait_send()
        return carry

    lax.fori_loop(0, HOPS, drain, 0)
    for q in range(1, 8):
        cot_copy(q).wait_send()


def on_device(counts, cotangent, saved_gate, saved_up, down_weight):
    tok, ff = saved_gate.shape
    d = cotangent.shape[1]
    vmem = pl.BlockSpec(memory_space=pltpu.VMEM)
    dma = pltpu.SemaphoreType.DMA
    n = len(CYCLES)
    return pl.pallas_call(
        kernel,
        out_shape=(
            jax.ShapeDtypeStruct((tok, ff), jnp.bfloat16),
            jax.ShapeDtypeStruct((tok, ff), jnp.bfloat16),
            jax.ShapeDtypeStruct((ff, d), jnp.bfloat16),
        ),
        in_specs=[
            pl.BlockSpec(memory_space=pltpu.SMEM), vmem, vmem, vmem, pl.BlockSpec(memory_space=pl.ANY),
        ],
        out_specs=(vmem, vmem, vmem),
        scratch_shapes=[
            pltpu.VMEM((ff, d), jnp.bfloat16),
            pltpu.VMEM((GROUPS, tok, d), jnp.bfloat16),
            pltpu.VMEM((GROUPS, ff, tok), jnp.bfloat16),
            pltpu.VMEM((GROUPS, TILES, tok, LANES), jnp.float32),
            pltpu.VMEM((2, HOPS, TILES, tok, LANES), jnp.bfloat16),
            pltpu.VMEM((2, HOPS, TILES, tok, LANES), jnp.bfloat16),
            dma, dma((8,)), dma((8,)), dma((8,)), dma((8,)),
            dma((n, 2, HOPS)), dma((n, 2, HOPS)), dma((n, 2, HOPS)), dma((n, 2, HOPS)),
        ],
        compiler_params=pltpu.CompilerParams(
            collective_id=0, has_side_effects=True, vmem_limit_bytes=60 * 2**20
        ),
        cost_estimate=pl.CostEstimate(
            flops=4 * GROUPS * tok * ff * d, bytes_accessed=4 * ff * d + 8 * tok * ff, transcendentals=2 * tok * ff
        ),
        name="down_backward",
    )(counts, cotangent, saved_gate, saved_up, down_weight)


def solution(mesh):
    return jax.shard_map(
        on_device,
        mesh=mesh,
        in_specs=(P(), P("col", "row"), P("row", "col"), P("row", "col"), P("col", "row")),
        out_specs=(P("row", "col"), P("row", "col"), P("col", "row")),
        check_vma=False,
    )
```

```python
import functools

import jax
import jax.numpy as jnp
from jax import lax
from jax.experimental import pallas as pl
from jax.experimental.pallas import tpu as pltpu
from jax.sharding import PartitionSpec as P

MESH = pl.DeviceIdType.MESH
GROUPS = 16
TOK = 128
LANES = 128
HOPS = 8
HALF = 64


def streams(*rows):
    first, out = 0, []
    for kind, cut, longer, count in rows:
        out.append((kind, cut, longer, first, count))
        first += count
    return tuple(out)


GATHER = streams(
    ("zig", 1, 0, 4), ("zig", 0, 0, 3), ("zig", 0, 1, 3), ("zig", 1, 1, 2),
    ("loop", 1, 1, 2), ("loop", 2, 1, 2), ("loop", 3, 0, 2), ("loop", 4, 0, 2),
    ("loop", 6, 0, 2), ("loop", 7, 1, 2), ("loop", 0, 0, 1), ("loop", 5, 1, 1),
)
SCATTER = streams(
    ("zig", 0, 0, 4), ("zig", 1, 1, 4), ("zig", 0, 1, 3), ("zig", 1, 0, 3),
    ("loop", 1, 0, 2), ("loop", 3, 0, 2), ("loop", 5, 1, 2), ("loop", 7, 0, 2),
    ("loop", 0, 1, 1), ("loop", 2, 1, 1), ("loop", 4, 1, 1), ("loop", 6, 1, 1),
)
TILES = 13
SOURCES = ((0, 0), (1, 0), (0, 1), (0, 3), (0, 2), (1, 1), (1, 3), (1, 2))


def place(cycle, p):
    kind, cut = cycle[:2]
    p = lax.rem(p + 2 * GROUPS, GROUPS)
    if kind == "zig":
        z = p // 2
        x = lax.rem(p + z + cut, 2)
        return x * 8 + z
    x = p // 8
    z = x * (15 - p) + (1 - x) * p
    return x * 8 + lax.rem(z + cut + 1, 8)


def spot(cycle, row):
    kind, cut = cycle[:2]
    x = row // 8
    z = lax.rem(row, 8)
    if kind == "zig":
        return 2 * z + lax.rem(x + z + cut, 2)
    z = lax.rem(z + 15 - cut, 8)
    return x * (15 - z) + (1 - x) * z


def hops_of(cycle, d):
    return HOPS if d == cycle[2] else HOPS - 1


def kernel(
    counts_ref, cot_ref, gate_ref, up_ref, weight_hbm,
    grad_gate_ref, grad_up_ref, grad_down_ref,
    weight, cot, hid, part, stage, arrived, factors, down_out,
    weight_sem, down_sem, cot_send, cot_recv, core_send, core_recv,
    hid_send, hid_recv, sum_send, sum_recv,
):
    row = lax.axis_index("row")
    col = lax.axis_index("col")
    x, z = row // 8, lax.rem(row, 8)
    xh = col // 8
    y = lax.rem(col // 2, 4)
    core = lax.rem(col, 2)

    def at_col(dx, dy, c):
        return lax.rem(xh + dx, 2) * 8 + lax.rem(y + dy, 4) * 2 + c

    load_weight = pltpu.make_async_copy(weight_hbm, weight, weight_sem)
    load_weight.start()

    barrier = pltpu.get_barrier_semaphore()
    rows = [(1 - x) * 8 + z, x * 8 + lax.rem(z + 1, 8), x * 8 + lax.rem(z + 7, 8)]
    cols = [at_col(0, 0, 1 - core)] + [at_col(dx, dy, core) for dx, dy in SOURCES[1:5]]
    for other in rows:
        pl.semaphore_signal(barrier, inc=1, device_id={"row": other}, device_id_type=MESH)
    for other in cols:
        pl.semaphore_signal(barrier, inc=1, device_id={"col": other}, device_id_type=MESH)

    limit = counts_ref[col]
    token = lax.broadcasted_iota(jnp.int32, cot_ref.shape, 0)
    cot[col] = jnp.where(token < limit, cot_ref[...], jnp.zeros_like(cot_ref))
    for t in range(TILES):
        lanes = pl.ds(t * LANES, LANES)
        g = gate_ref[:, lanes].astype(jnp.float32)
        u = up_ref[:, lanes].astype(jnp.float32)
        hid[row, lanes, :] = (g * jax.nn.sigmoid(g) * u).T.astype(jnp.bfloat16)
    pl.semaphore_wait(barrier, len(rows) + len(cols))

    def cot_copy(q):
        dx, dy = SOURCES[q]
        block = cot.at[at_col(dx if dy else 0, 0, core)]
        target = at_col(0, 4 - dy, core) if dy else at_col(1, 0, core)
        return pltpu.make_async_remote_copy(
            src_ref=block, dst_ref=block, send_sem=cot_send.at[q], recv_sem=cot_recv.at[q],
            device_id={"col": target}, device_id_type=MESH,
        )

    def source(q):
        dx = jnp.where((q == 1) | (q > 4), 1, 0)
        dy = jnp.where((q == 2) | (q == 5), 1, 0) + jnp.where((q == 3) | (q == 6), 3, 0)
        dy = dy + jnp.where((q == 4) | (q == 7), 2, 0)
        return dx, dy

    def core_copy(q):
        dx, dy = source(q)
        block = cot.at[at_col(dx, dy, core)]
        return pltpu.make_async_remote_copy(
            src_ref=block, dst_ref=block, send_sem=core_send.at[q], recv_sem=core_recv.at[q],
            device_id={"col": at_col(0, 0, 1 - core)}, device_id_type=MESH,
        )

    def core_arrival(q):
        dx, dy = source(q)
        block = cot.at[at_col(dx, dy, 1 - core)]
        return pltpu.make_async_remote_copy(
            src_ref=block, dst_ref=block, send_sem=core_send.at[q], recv_sem=core_recv.at[q],
            device_id={"col": at_col(0, 0, 1 - core)}, device_id_type=MESH,
        )

    def cot_arrival(q):
        dx, dy = source(q)
        block = cot.at[at_col(dx, dy, core)]
        return pltpu.make_async_remote_copy(
            src_ref=block, dst_ref=block, send_sem=cot_send.at[q], recv_sem=cot_recv.at[q],
            device_id={"col": at_col(0, 0, 1 - core)}, device_id_type=MESH,
        )

    def hid_copy(i, d, s, shift=0):
        cycle = GATHER[i]
        p = spot(cycle, row)
        way = 1 - 2 * d
        block = hid.at[
            place(cycle, p - way * (s + shift)),
            pl.ds(cycle[3] * HALF, cycle[4] * HALF),
        ]
        return pltpu.make_async_remote_copy(
            src_ref=block, dst_ref=block, send_sem=hid_send.at[i, d, s], recv_sem=hid_recv.at[i, d, s],
            device_id={"row": place(cycle, p + way)}, device_id_type=MESH,
        )

    def sum_copy(i, d, s):
        cycle = SCATTER[i]
        tiles = pl.ds(cycle[3], cycle[4])
        return pltpu.make_async_remote_copy(
            src_ref=stage.at[d, s, tiles], dst_ref=arrived.at[d, s, tiles],
            send_sem=sum_send.at[i, d, s], recv_sem=sum_recv.at[i, d, s],
            device_id={"row": place(cycle, spot(cycle, row) + 1 - 2 * d)}, device_id_type=MESH,
        )

    def each(walks, s, run):
        for i, cycle in enumerate(walks):
            for d in range(2):
                if hops_of(cycle, d) < HOPS:
                    pl.when(s < HOPS - 1)(lambda i=i, d=d: run(i, d))
                else:
                    run(i, d)

    for q in range(1, 5):
        cot_copy(q).start()
    core_copy(0).start()

    def gather_step(s, carry):
        @pl.when(s < HOPS)
        def _():
            def run(i, d):
                @pl.when(s > 0)
                def _():
                    hid_copy(i, d, s - 1, 1).wait_recv()

                hid_copy(i, d, s).start()

            each(GATHER, s, run)

        @pl.when((s > 0) & (s < HOPS))
        def _():
            cot_arrival(s).wait_recv()
            core_copy(s).start()

        @pl.when(s == 1)
        def _():
            for q in range(5, 8):
                cot_copy(q).start()
            load_weight.wait()

        @pl.when(s > 0)
        def _():
            core_arrival(s - 1).wait_recv()
            dx, dy = source(s - 1)
            first = at_col(dx, dy, 0)
            block = cot[pl.ds(first, 2)].reshape(2 * TOK, cot.shape[2])
            for t in range(0, TILES, 2):
                n = min(2, TILES - t)
                product = lax.dot_general(
                    block, weight[t * LANES:(t + n) * LANES, :], (((1,), (1,)), ((), ())),
                    preferred_element_type=jnp.float32,
                )
                for k in range(n):
                    piece = product[:, k * LANES:(k + 1) * LANES]
                    part[pl.ds(first, 2), 2 * (t + k):2 * (t + k) + 2] = piece.reshape(2, 2, HALF, LANES)

        return carry

    lax.fori_loop(0, HOPS + 1, gather_step, 0)

    def sum_send_step(s, received):
        def run(i, d):
            cycle = SCATTER[i]
            tiles = pl.ds(cycle[3], cycle[4])
            owner = place(cycle, spot(cycle, row) + (1 - 2 * d) * (hops_of(cycle, d) - s))
            value = part[owner, tiles]
            if received:
                sum_copy(i, d, s - 1).wait_recv()
                value = value + arrived[d, s - 1, tiles].astype(jnp.float32)
            stage[d, s, tiles] = value.astype(jnp.bfloat16)
            sum_copy(i, d, s).start()

        each(SCATTER, s, run)

    sum_send_step(0, False)
    for i, cycle in enumerate(GATHER):
        for d in range(2):
            hid_copy(i, d, hops_of(cycle, d) - 1, 1).wait_recv()

    def down(first, n):
        lhs = jnp.concatenate([hid[g, pl.ds(first, n), :] for g in range(GROUPS)], axis=1)
        down_out[pl.ds(first, n), :] = jnp.dot(
            lhs, cot[...].reshape(GROUPS * TOK, cot.shape[2]), preferred_element_type=jnp.float32
        ).astype(jnp.bfloat16)

    def sum_step(s, carry):
        sum_send_step(s, True)

        @pl.when(s < HOPS - 1)
        def _():
            down(pl.multiple_of((s - 1) * 2 * LANES, 2 * LANES), 2 * LANES)

        return carry

    lax.fori_loop(1, HOPS, sum_step, 0)
    down((TILES - 1) * LANES, LANES)

    store_down = pltpu.make_async_copy(down_out, grad_down_ref, down_sem)
    store_down.start()

    for t in range(TILES):
        lanes = pl.ds(t * LANES, LANES)
        g = gate_ref[:, lanes].astype(jnp.float32)
        u = up_ref[:, lanes].astype(jnp.float32)
        sig = jax.nn.sigmoid(g)
        factors[0, t] = g * sig
        factors[1, t] = u * (sig * (1.0 + g * (1.0 - sig)))

    for i, cycle in enumerate(SCATTER):
        tiles = pl.ds(cycle[3], cycle[4])
        total = part[row, tiles]
        for d in range(2):
            sum_copy(i, d, hops_of(cycle, d) - 1).wait_recv()
            total = total + arrived[d, hops_of(cycle, d) - 1, tiles].astype(jnp.float32)
        part[row, tiles] = total
    for t in range(TILES):
        lanes = pl.ds(t * LANES, LANES)
        grad = part[row, 2 * t:2 * t + 2].reshape(TOK, LANES)
        grad_up_ref[:, lanes] = (grad * factors[0, t]).astype(jnp.bfloat16)
        grad_gate_ref[:, lanes] = (grad * factors[1, t]).astype(jnp.bfloat16)

    def drain(s, carry):
        each(GATHER, s, lambda i, d: hid_copy(i, d, s).wait_send())
        each(SCATTER, s, lambda i, d: sum_copy(i, d, s).wait_send())
        core_copy(s).wait_send()
        return carry

    lax.fori_loop(0, HOPS, drain, 0)
    for q in range(1, 8):
        cot_copy(q).wait_send()
    store_down.wait()


def copy_kernel(pieces, *refs):
    n = len(refs) // 3
    take, give = refs[-2], refs[-1]
    steps, k = [], 0
    for a in range(n):
        source, target, held = refs[a], refs[n + a], refs[2 * n + a]
        rows = source.shape[0] // pieces[a]
        for p in range(pieces[a]):
            part = pl.ds(p * rows, rows)
            steps.append((
                pltpu.make_async_copy(source.at[part], held.at[part], take.at[k]),
                pltpu.make_async_copy(held.at[part], target.at[part], give.at[k]),
            ))
            k += 1
    for step in steps:
        step[0].start()
    for step in steps:
        step[0].wait()
        step[1].start()
    for step in steps:
        step[1].wait()


def copied(pieces, *arrays):
    anywhere = pl.BlockSpec(memory_space=pl.ANY)
    sems = pltpu.SemaphoreType.DMA((sum(pieces),))
    return pl.pallas_call(
        functools.partial(copy_kernel, pieces),
        out_shape=tuple(jax.ShapeDtypeStruct(a.shape, a.dtype) for a in arrays),
        in_specs=[anywhere] * len(arrays),
        out_specs=(anywhere,) * len(arrays),
        scratch_shapes=[pltpu.VMEM(a.shape, a.dtype) for a in arrays] + [sems, sems],
        compiler_params=pltpu.CompilerParams(vmem_limit_bytes=16 * 2**20),
        name="copy_out",
    )(*arrays)


def on_device(counts, cotangent, saved_gate, saved_up, down_weight):
    tok, ff = saved_gate.shape
    d = cotangent.shape[1]
    vmem = pl.BlockSpec(memory_space=pltpu.VMEM)
    dma = pltpu.SemaphoreType.DMA
    results = pl.pallas_call(
        kernel,
        out_shape=(
            jax.ShapeDtypeStruct((tok, ff), jnp.bfloat16),
            jax.ShapeDtypeStruct((tok, ff), jnp.bfloat16),
            jax.ShapeDtypeStruct((ff, d), jnp.bfloat16),
        ),
        in_specs=[
            pl.BlockSpec(memory_space=pltpu.SMEM), vmem, vmem, vmem, pl.BlockSpec(memory_space=pl.ANY),
        ],
        out_specs=(vmem, vmem, pl.BlockSpec(memory_space=pl.ANY)),
        scratch_shapes=[
            pltpu.VMEM((ff, d), jnp.bfloat16),
            pltpu.VMEM((GROUPS, tok, d), jnp.bfloat16),
            pltpu.VMEM((GROUPS, ff, tok), jnp.bfloat16),
            pltpu.VMEM((GROUPS, 2 * TILES, HALF, LANES), jnp.float32),
            pltpu.VMEM((2, HOPS, 2 * TILES, HALF, LANES), jnp.bfloat16),
            pltpu.VMEM((2, HOPS, 2 * TILES, HALF, LANES), jnp.bfloat16),
            pltpu.VMEM((2, TILES, tok, LANES), jnp.float32),
            pltpu.VMEM((ff, d), jnp.bfloat16),
            dma, dma, dma((8,)), dma((8,)), dma((8,)), dma((8,)),
            dma((len(GATHER), 2, HOPS)), dma((len(GATHER), 2, HOPS)),
            dma((len(SCATTER), 2, HOPS)), dma((len(SCATTER), 2, HOPS)),
        ],
        compiler_params=pltpu.CompilerParams(
            collective_id=0, has_side_effects=True, vmem_limit_bytes=60 * 2**20
        ),
        cost_estimate=pl.CostEstimate(
            flops=4 * GROUPS * tok * ff * d, bytes_accessed=4 * ff * d + 8 * tok * ff, transcendentals=2 * tok * ff
        ),
        name="down_backward",
    )(counts, cotangent, saved_gate, saved_up, down_weight)
    return copied((1, 1, 4), *results)


def solution(mesh):
    return jax.shard_map(
        on_device,
        mesh=mesh,
        in_specs=(P(), P("col", "row"), P("row", "col"), P("row", "col"), P("col", "row")),
        out_specs=(P("row", "col"), P("row", "col"), P("col", "row")),
        check_vma=False,
    )
```

```python
import functools

import jax
import jax.numpy as jnp
from jax import lax
from jax.experimental import pallas as pl
from jax.experimental.pallas import tpu as pltpu
from jax.sharding import PartitionSpec as P

MESH = pl.DeviceIdType.MESH
GROUPS = 16
TOK = 128
LANES = 128
HOPS = 8
HALF = 64


def streams(*rows):
    first, out = 0, []
    for kind, cut, longer, count in rows:
        out.append((kind, cut, longer, first, count))
        first += count
    return tuple(out)


GATHER = streams(
    ("zig", 1, 0, 4), ("zig", 0, 1, 3), ("loop", 1, 1, 2), ("loop", 3, 0, 2), ("loop", 6, 0, 2), ("loop", 0, 0, 1),
    ("zig", 0, 0, 3), ("zig", 1, 1, 2), ("loop", 2, 1, 2), ("loop", 4, 0, 2), ("loop", 7, 1, 2), ("loop", 5, 1, 1),
)
SCATTER = streams(
    ("zig", 0, 0, 4), ("zig", 1, 1, 4), ("loop", 1, 0, 2), ("loop", 5, 1, 2), ("loop", 0, 1, 1), ("loop", 4, 1, 1),
    ("zig", 0, 1, 3), ("zig", 1, 0, 3), ("loop", 3, 0, 2), ("loop", 7, 0, 2), ("loop", 2, 1, 1), ("loop", 6, 1, 1),
)
SETS = (range(0, 6), range(6, 12))
TILES = 13
SOURCES = ((0, 0), (1, 0), (0, 1), (0, 3), (0, 2), (1, 1), (1, 3), (1, 2))


def place(cycle, p):
    kind, cut = cycle[:2]
    p = lax.rem(p + 2 * GROUPS, GROUPS)
    if kind == "zig":
        z = p // 2
        x = lax.rem(p + z + cut, 2)
        return x * 8 + z
    x = p // 8
    z = x * (15 - p) + (1 - x) * p
    return x * 8 + lax.rem(z + cut + 1, 8)


def spot(cycle, row):
    kind, cut = cycle[:2]
    x = row // 8
    z = lax.rem(row, 8)
    if kind == "zig":
        return 2 * z + lax.rem(x + z + cut, 2)
    z = lax.rem(z + 15 - cut, 8)
    return x * (15 - z) + (1 - x) * z


def hops_of(cycle, d):
    return HOPS if d == cycle[2] else HOPS - 1


def kernel(
    counts_ref, cot_hbm, gate_hbm, up_hbm, weight_hbm,
    grad_gate_ref, grad_up_ref, grad_down_ref,
    cot_ref, gate_ref, up_ref, weight, cot, hid, part, stage, arrived, factors, down_out,
    load_sem, down_sem, cot_send, cot_recv, core_send, core_recv,
    hid_send, hid_recv, sum_send, sum_recv,
):
    row = lax.axis_index("row")
    col = lax.axis_index("col")
    x, z = row // 8, lax.rem(row, 8)
    xh = col // 8
    y = lax.rem(col // 2, 4)
    core = lax.rem(col, 2)

    def at_col(dx, dy, c):
        return lax.rem(xh + dx, 2) * 8 + lax.rem(y + dy, 4) * 2 + c

    pairs = ((cot_hbm, cot_ref), (gate_hbm, gate_ref), (up_hbm, up_ref), (weight_hbm, weight))
    loads = [pltpu.make_async_copy(*pair, load_sem.at[k]) for k, pair in enumerate(pairs)]
    for load in loads:
        load.start()

    barrier = pltpu.get_barrier_semaphore()
    rows = [(1 - x) * 8 + z, x * 8 + lax.rem(z + 1, 8), x * 8 + lax.rem(z + 7, 8)]
    cols = [at_col(0, 0, 1 - core)] + [at_col(dx, dy, core) for dx, dy in SOURCES[1:5]]
    for other in rows:
        pl.semaphore_signal(barrier, inc=1, device_id={"row": other}, device_id_type=MESH)
    for other in cols:
        pl.semaphore_signal(barrier, inc=1, device_id={"col": other}, device_id_type=MESH)

    limit = counts_ref[col]
    token = lax.broadcasted_iota(jnp.int32, cot_ref.shape, 0)
    loads[0].wait()
    cot[col] = jnp.where(token < limit, cot_ref[...], jnp.zeros_like(cot_ref))
    pl.semaphore_wait(barrier, len(rows) + len(cols))

    def cot_copy(q):
        dx, dy = SOURCES[q]
        block = cot.at[at_col(dx if dy else 0, 0, core)]
        target = at_col(0, 4 - dy, core) if dy else at_col(1, 0, core)
        return pltpu.make_async_remote_copy(
            src_ref=block, dst_ref=block, send_sem=cot_send.at[q], recv_sem=cot_recv.at[q],
            device_id={"col": target}, device_id_type=MESH,
        )

    def source(q):
        dx = jnp.where((q == 1) | (q > 4), 1, 0)
        dy = jnp.where((q == 2) | (q == 5), 1, 0) + jnp.where((q == 3) | (q == 6), 3, 0)
        dy = dy + jnp.where((q == 4) | (q == 7), 2, 0)
        return dx, dy

    def core_copy(q):
        dx, dy = source(q)
        block = cot.at[at_col(dx, dy, core)]
        return pltpu.make_async_remote_copy(
            src_ref=block, dst_ref=block, send_sem=core_send.at[q], recv_sem=core_recv.at[q],
            device_id={"col": at_col(0, 0, 1 - core)}, device_id_type=MESH,
        )

    def core_arrival(q):
        dx, dy = source(q)
        block = cot.at[at_col(dx, dy, 1 - core)]
        return pltpu.make_async_remote_copy(
            src_ref=block, dst_ref=block, send_sem=core_send.at[q], recv_sem=core_recv.at[q],
            device_id={"col": at_col(0, 0, 1 - core)}, device_id_type=MESH,
        )

    def cot_arrival(q):
        dx, dy = source(q)
        block = cot.at[at_col(dx, dy, core)]
        return pltpu.make_async_remote_copy(
            src_ref=block, dst_ref=block, send_sem=cot_send.at[q], recv_sem=cot_recv.at[q],
            device_id={"col": at_col(0, 0, 1 - core)}, device_id_type=MESH,
        )

    def hid_copy(i, d, s, shift=0):
        cycle = GATHER[i]
        p = spot(cycle, row)
        way = 1 - 2 * d
        block = hid.at[
            place(cycle, p - way * (s + shift)),
            pl.ds(cycle[3] * HALF, cycle[4] * HALF),
        ]
        return pltpu.make_async_remote_copy(
            src_ref=block, dst_ref=block, send_sem=hid_send.at[i, d, s], recv_sem=hid_recv.at[i, d, s],
            device_id={"row": place(cycle, p + way)}, device_id_type=MESH,
        )

    def sum_copy(i, d, s):
        cycle = SCATTER[i]
        tiles = pl.ds(cycle[3], cycle[4])
        return pltpu.make_async_remote_copy(
            src_ref=stage.at[d, s, tiles], dst_ref=arrived.at[d, s, tiles],
            send_sem=sum_send.at[i, d, s], recv_sem=sum_recv.at[i, d, s],
            device_id={"row": place(cycle, spot(cycle, row) + 1 - 2 * d)}, device_id_type=MESH,
        )

    def each(walks, s, run, picks=range(12)):
        for i in picks:
            cycle = walks[i]
            for d in range(2):
                if hops_of(cycle, d) < HOPS:
                    pl.when(s < HOPS - 1)(lambda i=i, d=d: run(i, d))
                else:
                    run(i, d)

    for q in range(1, 5):
        cot_copy(q).start()
    core_copy(0).start()

    loads[1].wait()
    loads[2].wait()
    tiles_done = 0
    for i, cycle in enumerate(GATHER):
        while 2 * tiles_done < cycle[3] + cycle[4]:
            lanes = pl.ds(tiles_done * LANES, LANES)
            g = gate_ref[:, lanes].astype(jnp.float32)
            u = up_ref[:, lanes].astype(jnp.float32)
            hid[row, lanes, :] = (g * jax.nn.sigmoid(g) * u).T.astype(jnp.bfloat16)
            tiles_done += 1
        for d in range(2):
            hid_copy(i, d, 0).start()
    loads[3].wait()

    def pass_on(s, picks):
        def run(i, d):
            hid_copy(i, d, s - 1, 1).wait_recv()
            hid_copy(i, d, s).start()

        each(GATHER, s, run, picks)

    def partial_sums(q, carry):
        core_arrival(q).wait_recv()
        dx, dy = source(q)
        first = at_col(dx, dy, 0)
        block = cot[pl.ds(first, 2)].reshape(2 * TOK, cot.shape[2])
        for t in range(0, TILES, 2):
            n = min(2, TILES - t)
            product = lax.dot_general(
                block, weight[t * LANES:(t + n) * LANES, :], (((1,), (1,)), ((), ())),
                preferred_element_type=jnp.float32,
            )
            for k in range(n):
                piece = product[:, k * LANES:(k + 1) * LANES]
                part[pl.ds(first, 2), 2 * (t + k):2 * (t + k) + 2] = piece.reshape(2, 2, HALF, LANES)
        return carry

    def across(q, carry):
        cot_arrival(q).wait_recv()
        core_copy(q).start()
        return carry

    def after(s):
        return lax.div(3 * s + 2, 2)

    def gather_step(s, carry):
        pass_on(s, SETS[0])

        @pl.when(s < 6)
        def _():
            lax.fori_loop(after(s - 1), after(s), across, 0)

        @pl.when(s == 1)
        def _():
            for q in range(5, 8):
                cot_copy(q).start()

        lax.fori_loop(jnp.where(s == 1, 0, after(s - 2)), after(s - 1), partial_sums, 0)
        pass_on(s, SETS[1])
        return carry

    lax.fori_loop(1, HOPS - 1, gather_step, 0)

    def sum_send_step(s, received, picks):
        def run(i, d):
            cycle = SCATTER[i]
            tiles = pl.ds(cycle[3], cycle[4])
            owner = place(cycle, spot(cycle, row) + (1 - 2 * d) * (hops_of(cycle, d) - s))
            value = part[owner, tiles]
            if received:
                sum_copy(i, d, s - 1).wait_recv()
                value = value + arrived[d, s - 1, tiles].astype(jnp.float32)
            stage[d, s, tiles] = value.astype(jnp.bfloat16)
            sum_copy(i, d, s).start()

        each(SCATTER, s, run, picks)

    for picks in SETS:
        sum_send_step(0, False, picks)
        pass_on(HOPS - 1, picks)

    def down(first, n):
        lhs = jnp.concatenate([hid[g, pl.ds(first, n), :] for g in range(GROUPS)], axis=1)
        down_out[pl.ds(first, n), :] = jnp.dot(
            lhs, cot[...].reshape(GROUPS * TOK, cot.shape[2]), preferred_element_type=jnp.float32
        ).astype(jnp.bfloat16)

    def down_piece(k, carry):
        down(pl.multiple_of(k * 2 * LANES, 2 * LANES), 2 * LANES)
        return carry

    def sum_step(s, carry):
        sum_send_step(s, True, SETS[0])

        @pl.when(s == 1)
        def _():
            for i, cycle in enumerate(GATHER):
                for d in range(2):
                    hid_copy(i, d, hops_of(cycle, d) - 1, 1).wait_recv()

        @pl.when(s > 1)
        def _():
            down_piece(s - 2, 0)

        sum_send_step(s, True, SETS[1])
        return carry

    lax.fori_loop(1, HOPS, sum_step, 0)
    down((TILES - 1) * LANES, LANES)

    store_down = pltpu.make_async_copy(down_out, grad_down_ref, down_sem)
    store_down.start()

    for t in range(TILES):
        lanes = pl.ds(t * LANES, LANES)
        g = gate_ref[:, lanes].astype(jnp.float32)
        u = up_ref[:, lanes].astype(jnp.float32)
        sig = jax.nn.sigmoid(g)
        factors[0, t] = g * sig
        factors[1, t] = u * (sig * (1.0 + g * (1.0 - sig)))

    for i, cycle in enumerate(SCATTER):
        tiles = pl.ds(cycle[3], cycle[4])
        total = part[row, tiles]
        for d in range(2):
            sum_copy(i, d, hops_of(cycle, d) - 1).wait_recv()
            total = total + arrived[d, hops_of(cycle, d) - 1, tiles].astype(jnp.float32)
        part[row, tiles] = total
    for t in range(TILES):
        lanes = pl.ds(t * LANES, LANES)
        grad = part[row, 2 * t:2 * t + 2].reshape(TOK, LANES)
        grad_up_ref[:, lanes] = (grad * factors[0, t]).astype(jnp.bfloat16)
        grad_gate_ref[:, lanes] = (grad * factors[1, t]).astype(jnp.bfloat16)

    def drain(s, carry):
        each(GATHER, s, lambda i, d: hid_copy(i, d, s).wait_send())
        each(SCATTER, s, lambda i, d: sum_copy(i, d, s).wait_send())
        core_copy(s).wait_send()
        return carry

    lax.fori_loop(0, HOPS, drain, 0)
    for q in range(1, 8):
        cot_copy(q).wait_send()
    store_down.wait()


def copy_kernel(pieces, *refs):
    n = len(refs) // 3
    take, give = refs[-2], refs[-1]
    steps, k = [], 0
    for a in range(n):
        source, target, held = refs[a], refs[n + a], refs[2 * n + a]
        rows = source.shape[0] // pieces[a]
        for p in range(pieces[a]):
            part = pl.ds(p * rows, rows)
            steps.append((
                pltpu.make_async_copy(source.at[part], held.at[part], take.at[k]),
                pltpu.make_async_copy(held.at[part], target.at[part], give.at[k]),
            ))
            k += 1
    for step in steps:
        step[0].start()
    for step in steps:
        step[0].wait()
        step[1].start()
    for step in steps:
        step[1].wait()


def copied(pieces, *arrays):
    anywhere = pl.BlockSpec(memory_space=pl.ANY)
    sems = pltpu.SemaphoreType.DMA((sum(pieces),))
    return pl.pallas_call(
        functools.partial(copy_kernel, pieces),
        out_shape=tuple(jax.ShapeDtypeStruct(a.shape, a.dtype) for a in arrays),
        in_specs=[anywhere] * len(arrays),
        out_specs=(anywhere,) * len(arrays),
        scratch_shapes=[pltpu.VMEM(a.shape, a.dtype) for a in arrays] + [sems, sems],
        compiler_params=pltpu.CompilerParams(vmem_limit_bytes=60 * 2**20),
        name="copy_out",
    )(*arrays)


def on_device(counts, cotangent, saved_gate, saved_up, down_weight):
    tok, ff = saved_gate.shape
    d = cotangent.shape[1]
    vmem = pl.BlockSpec(memory_space=pltpu.VMEM)
    anywhere = pl.BlockSpec(memory_space=pl.ANY)
    dma = pltpu.SemaphoreType.DMA
    results = pl.pallas_call(
        kernel,
        out_shape=(
            jax.ShapeDtypeStruct((tok, ff), jnp.bfloat16),
            jax.ShapeDtypeStruct((tok, ff), jnp.bfloat16),
            jax.ShapeDtypeStruct((ff, d), jnp.bfloat16),
        ),
        in_specs=[
            pl.BlockSpec(memory_space=pltpu.SMEM), anywhere, anywhere, anywhere, anywhere,
        ],
        out_specs=(vmem, vmem, anywhere),
        scratch_shapes=[
            pltpu.VMEM((tok, d), jnp.bfloat16),
            pltpu.VMEM((tok, ff), jnp.bfloat16),
            pltpu.VMEM((tok, ff), jnp.bfloat16),
            pltpu.VMEM((ff, d), jnp.bfloat16),
            pltpu.VMEM((GROUPS, tok, d), jnp.bfloat16),
            pltpu.VMEM((GROUPS, ff, tok), jnp.bfloat16),
            pltpu.VMEM((GROUPS, 2 * TILES, HALF, LANES), jnp.float32),
            pltpu.VMEM((2, HOPS, 2 * TILES, HALF, LANES), jnp.bfloat16),
            pltpu.VMEM((2, HOPS, 2 * TILES, HALF, LANES), jnp.bfloat16),
            pltpu.VMEM((2, TILES, tok, LANES), jnp.float32),
            pltpu.VMEM((ff, d), jnp.bfloat16),
            dma((4,)), dma, dma((8,)), dma((8,)), dma((8,)), dma((8,)),
            dma((len(GATHER), 2, HOPS)), dma((len(GATHER), 2, HOPS)),
            dma((len(SCATTER), 2, HOPS)), dma((len(SCATTER), 2, HOPS)),
        ],
        compiler_params=pltpu.CompilerParams(
            collective_id=0, has_side_effects=True, vmem_limit_bytes=60 * 2**20
        ),
        cost_estimate=pl.CostEstimate(
            flops=4 * GROUPS * tok * ff * d, bytes_accessed=4 * ff * d + 8 * tok * ff, transcendentals=2 * tok * ff
        ),
        name="down_backward",
    )(counts, cotangent, saved_gate, saved_up, down_weight)
    return copied((1, 1, 4), *results)


def solution(mesh):
    return jax.shard_map(
        on_device,
        mesh=mesh,
        in_specs=(P(), P("col", "row"), P("row", "col"), P("row", "col"), P("col", "row")),
        out_specs=(P("row", "col"), P("row", "col"), P("col", "row")),
        check_vma=False,
    )
```

```python
import functools

import jax
import jax.numpy as jnp
from jax import lax
from jax.experimental import pallas as pl
from jax.experimental.pallas import tpu as pltpu
from jax.sharding import PartitionSpec as P

MESH = pl.DeviceIdType.MESH
GROUPS = 16
TOK = 128
LANES = 128
HOPS = 8
HALF = 64


def streams(*rows):
    first, out = 0, []
    for kind, cut, longer, count in rows:
        out.append((kind, cut, longer, first, count))
        first += count
    return tuple(out)


GATHER = streams(
    ("zig", 1, 0, 4), ("zig", 0, 1, 3), ("loop", 1, 1, 2), ("loop", 3, 0, 2), ("loop", 6, 0, 2), ("loop", 0, 0, 1),
    ("zig", 0, 0, 3), ("zig", 1, 1, 2), ("loop", 2, 1, 2), ("loop", 4, 0, 2), ("loop", 7, 1, 2), ("loop", 5, 1, 1),
)
SCATTER = streams(
    ("zig", 0, 0, 4), ("zig", 1, 1, 4), ("loop", 1, 0, 2), ("loop", 5, 1, 2), ("loop", 0, 1, 1), ("loop", 4, 1, 1),
    ("zig", 0, 1, 3), ("zig", 1, 0, 3), ("loop", 3, 0, 2), ("loop", 7, 0, 2), ("loop", 2, 1, 1), ("loop", 6, 1, 1),
)
SETS = (range(0, 6), range(6, 12))
TILES = 13
SOURCES = ((0, 0), (1, 0), (0, 1), (0, 3), (0, 2), (1, 1), (1, 3), (1, 2))


def place(cycle, p):
    kind, cut = cycle[:2]
    p = lax.rem(p + 2 * GROUPS, GROUPS)
    if kind == "zig":
        z = p // 2
        x = lax.rem(p + z + cut, 2)
        return x * 8 + z
    x = p // 8
    z = x * (15 - p) + (1 - x) * p
    return x * 8 + lax.rem(z + cut + 1, 8)


def spot(cycle, row):
    kind, cut = cycle[:2]
    x = row // 8
    z = lax.rem(row, 8)
    if kind == "zig":
        return 2 * z + lax.rem(x + z + cut, 2)
    z = lax.rem(z + 15 - cut, 8)
    return x * (15 - z) + (1 - x) * z


def hops_of(cycle, d):
    return HOPS if d == cycle[2] else HOPS - 1


def kernel(
    counts_ref, cot_hbm, gate_hbm, up_hbm, weight_hbm,
    grad_gate_ref, grad_up_ref, grad_down_ref,
    cot_ref, gate_ref, up_ref, weight, cot, hid, part, stage, arrived, factors, down_out,
    load_sem, down_sem, cot_send, cot_recv, core_send, core_recv,
    hid_send, hid_recv, sum_send, sum_recv,
):
    row = lax.axis_index("row")
    col = lax.axis_index("col")
    x, z = row // 8, lax.rem(row, 8)
    xh = col // 8
    y = lax.rem(col // 2, 4)
    core = lax.rem(col, 2)

    def at_col(dx, dy, c):
        return lax.rem(xh + dx, 2) * 8 + lax.rem(y + dy, 4) * 2 + c

    pairs = ((cot_hbm, cot_ref), (gate_hbm, gate_ref), (up_hbm, up_ref), (weight_hbm, weight))
    loads = [pltpu.make_async_copy(*pair, load_sem.at[k]) for k, pair in enumerate(pairs)]
    for load in loads:
        load.start()

    barrier = pltpu.get_barrier_semaphore()
    rows = [(1 - x) * 8 + z, x * 8 + lax.rem(z + 1, 8), x * 8 + lax.rem(z + 7, 8)]
    cols = [at_col(0, 0, 1 - core)] + [at_col(dx, dy, core) for dx, dy in SOURCES[1:5]]
    for other in rows:
        pl.semaphore_signal(barrier, inc=1, device_id={"row": other}, device_id_type=MESH)
    for other in cols:
        pl.semaphore_signal(barrier, inc=1, device_id={"col": other}, device_id_type=MESH)

    limit = counts_ref[col]
    token = lax.broadcasted_iota(jnp.int32, cot_ref.shape, 0)
    loads[0].wait()
    cot[col] = jnp.where(token < limit, cot_ref[...], jnp.zeros_like(cot_ref))
    pl.semaphore_wait(barrier, len(rows) + len(cols))

    def cot_copy(q):
        dx, dy = SOURCES[q]
        block = cot.at[at_col(dx if dy else 0, 0, core)]
        target = at_col(0, 4 - dy, core) if dy else at_col(1, 0, core)
        return pltpu.make_async_remote_copy(
            src_ref=block, dst_ref=block, send_sem=cot_send.at[q], recv_sem=cot_recv.at[q],
            device_id={"col": target}, device_id_type=MESH,
        )

    def source(q):
        dx = jnp.where((q == 1) | (q > 4), 1, 0)
        dy = jnp.where((q == 2) | (q == 5), 1, 0) + jnp.where((q == 3) | (q == 6), 3, 0)
        dy = dy + jnp.where((q == 4) | (q == 7), 2, 0)
        return dx, dy

    def core_copy(q):
        dx, dy = source(q)
        block = cot.at[at_col(dx, dy, core)]
        return pltpu.make_async_remote_copy(
            src_ref=block, dst_ref=block, send_sem=core_send.at[q], recv_sem=core_recv.at[q],
            device_id={"col": at_col(0, 0, 1 - core)}, device_id_type=MESH,
        )

    def core_arrival(q):
        dx, dy = source(q)
        block = cot.at[at_col(dx, dy, 1 - core)]
        return pltpu.make_async_remote_copy(
            src_ref=block, dst_ref=block, send_sem=core_send.at[q], recv_sem=core_recv.at[q],
            device_id={"col": at_col(0, 0, 1 - core)}, device_id_type=MESH,
        )

    def cot_arrival(q):
        dx, dy = source(q)
        block = cot.at[at_col(dx, dy, core)]
        return pltpu.make_async_remote_copy(
            src_ref=block, dst_ref=block, send_sem=cot_send.at[q], recv_sem=cot_recv.at[q],
            device_id={"col": at_col(0, 0, 1 - core)}, device_id_type=MESH,
        )

    def hid_copy(i, d, s, shift=0):
        cycle = GATHER[i]
        p = spot(cycle, row)
        way = 1 - 2 * d
        block = hid.at[
            place(cycle, p - way * (s + shift)),
            pl.ds(cycle[3] * HALF, cycle[4] * HALF),
        ]
        return pltpu.make_async_remote_copy(
            src_ref=block, dst_ref=block, send_sem=hid_send, recv_sem=hid_recv.at[i, d, s],
            device_id={"row": place(cycle, p + way)}, device_id_type=MESH,
        )

    def sum_copy(i, d, s):
        cycle = SCATTER[i]
        tiles = pl.ds(cycle[3], cycle[4])
        return pltpu.make_async_remote_copy(
            src_ref=stage.at[d, s, tiles], dst_ref=arrived.at[d, s, tiles],
            send_sem=sum_send, recv_sem=sum_recv.at[i, d, s],
            device_id={"row": place(cycle, spot(cycle, row) + 1 - 2 * d)}, device_id_type=MESH,
        )

    def each(walks, s, run, picks=range(12)):
        for i in picks:
            cycle = walks[i]
            for d in range(2):
                if hops_of(cycle, d) < HOPS:
                    pl.when(s < HOPS - 1)(lambda i=i, d=d: run(i, d))
                else:
                    run(i, d)

    for q in range(1, 5):
        cot_copy(q).start()
    core_copy(0).start()

    loads[1].wait()
    loads[2].wait()
    tiles_done = 0
    for i, cycle in enumerate(GATHER):
        while 2 * tiles_done < cycle[3] + cycle[4]:
            lanes = pl.ds(tiles_done * LANES, LANES)
            g = gate_ref[:, lanes].astype(jnp.float32)
            u = up_ref[:, lanes].astype(jnp.float32)
            hid[row, lanes, :] = (g * jax.nn.sigmoid(g) * u).T.astype(jnp.bfloat16)
            tiles_done += 1
        for d in range(2):
            hid_copy(i, d, 0).start()
    loads[3].wait()

    def pass_on(s, picks):
        def run(i, d):
            hid_copy(i, d, s - 1, 1).wait_recv()
            hid_copy(i, d, s).start()

        each(GATHER, s, run, picks)

    def partial_sums(q, carry):
        core_arrival(q).wait_recv()
        dx, dy = source(q)
        first = at_col(dx, dy, 0)
        block = cot[pl.ds(first, 2)].reshape(2 * TOK, cot.shape[2])
        for t in range(0, TILES, 2):
            n = min(2, TILES - t)
            product = lax.dot_general(
                block, weight[t * LANES:(t + n) * LANES, :], (((1,), (1,)), ((), ())),
                preferred_element_type=jnp.float32,
            )
            for k in range(n):
                piece = product[:, k * LANES:(k + 1) * LANES]
                part[pl.ds(first, 2), 2 * (t + k):2 * (t + k) + 2] = piece.reshape(2, 2, HALF, LANES)
        return carry

    def across(q, carry):
        cot_arrival(q).wait_recv()
        core_copy(q).start()
        return carry

    def after(s):
        return lax.div(3 * s + 2, 2)

    def gather_step(s, carry):
        pass_on(s, SETS[0])

        @pl.when(s < 6)
        def _():
            lax.fori_loop(after(s - 1), after(s), across, 0)

        @pl.when(s == 1)
        def _():
            for q in range(5, 8):
                cot_copy(q).start()

        lax.fori_loop(jnp.where(s == 1, 0, after(s - 2)), after(s - 1), partial_sums, 0)
        pass_on(s, SETS[1])
        return carry

    lax.fori_loop(1, HOPS - 1, gather_step, 0)

    def sum_send_step(s, received, picks):
        def run(i, d):
            cycle = SCATTER[i]
            tiles = pl.ds(cycle[3], cycle[4])
            owner = place(cycle, spot(cycle, row) + (1 - 2 * d) * (hops_of(cycle, d) - s))
            value = part[owner, tiles]
            if received:
                sum_copy(i, d, s - 1).wait_recv()
                value = value + arrived[d, s - 1, tiles].astype(jnp.float32)
            stage[d, s, tiles] = value.astype(jnp.bfloat16)
            sum_copy(i, d, s).start()

        each(SCATTER, s, run, picks)

    for picks in SETS:
        sum_send_step(0, False, picks)
        pass_on(HOPS - 1, picks)

    def down(first, n):
        lhs = jnp.concatenate([hid[g, pl.ds(first, n), :] for g in range(GROUPS)], axis=1)
        down_out[pl.ds(first, n), :] = jnp.dot(
            lhs, cot[...].reshape(GROUPS * TOK, cot.shape[2]), preferred_element_type=jnp.float32
        ).astype(jnp.bfloat16)

    def down_piece(k, carry):
        down(pl.multiple_of(k * 2 * LANES, 2 * LANES), 2 * LANES)
        return carry

    def sum_step(s, carry):
        sum_send_step(s, True, SETS[0])

        @pl.when(s == 1)
        def _():
            for i, cycle in enumerate(GATHER):
                for d in range(2):
                    hid_copy(i, d, hops_of(cycle, d) - 1, 1).wait_recv()

        @pl.when(s > 1)
        def _():
            down_piece(s - 2, 0)

        sum_send_step(s, True, SETS[1])
        return carry

    lax.fori_loop(1, HOPS, sum_step, 0)
    down((TILES - 1) * LANES, LANES)

    store_down = pltpu.make_async_copy(down_out, grad_down_ref, down_sem)
    store_down.start()

    for t in range(TILES):
        lanes = pl.ds(t * LANES, LANES)
        g = gate_ref[:, lanes].astype(jnp.float32)
        u = up_ref[:, lanes].astype(jnp.float32)
        sig = jax.nn.sigmoid(g)
        factors[0, t] = g * sig
        factors[1, t] = u * (sig * (1.0 + g * (1.0 - sig)))

    for i, cycle in enumerate(SCATTER):
        tiles = pl.ds(cycle[3], cycle[4])
        total = part[row, tiles]
        for d in range(2):
            sum_copy(i, d, hops_of(cycle, d) - 1).wait_recv()
            total = total + arrived[d, hops_of(cycle, d) - 1, tiles].astype(jnp.float32)
        part[row, tiles] = total
    for t in range(TILES):
        lanes = pl.ds(t * LANES, LANES)
        grad = part[row, 2 * t:2 * t + 2].reshape(TOK, LANES)
        grad_up_ref[:, lanes] = (grad * factors[0, t]).astype(jnp.bfloat16)
        grad_gate_ref[:, lanes] = (grad * factors[1, t]).astype(jnp.bfloat16)

    blocks = hid.at[pl.ds(0, GROUPS - 1)]
    for sem in (hid_send, sum_send):
        pltpu.make_async_copy(blocks, blocks, sem).wait()
    for q in range(8):
        core_copy(q).wait_send()
    for q in range(1, 8):
        cot_copy(q).wait_send()
    store_down.wait()


def copy_kernel(pieces, *refs):
    n = len(refs) // 3
    take, give = refs[-2], refs[-1]
    steps, k = [], 0
    for a in range(n):
        source, target, held = refs[a], refs[n + a], refs[2 * n + a]
        rows = source.shape[0] // pieces[a]
        for p in range(pieces[a]):
            part = pl.ds(p * rows, rows)
            steps.append((
                pltpu.make_async_copy(source.at[part], held.at[part], take.at[k]),
                pltpu.make_async_copy(held.at[part], target.at[part], give.at[k]),
            ))
            k += 1
    for step in steps:
        step[0].start()
    for step in steps:
        step[0].wait()
        step[1].start()
    for step in steps:
        step[1].wait()


def copied(pieces, *arrays):
    anywhere = pl.BlockSpec(memory_space=pl.ANY)
    sems = pltpu.SemaphoreType.DMA((sum(pieces),))
    return pl.pallas_call(
        functools.partial(copy_kernel, pieces),
        out_shape=tuple(jax.ShapeDtypeStruct(a.shape, a.dtype) for a in arrays),
        in_specs=[anywhere] * len(arrays),
        out_specs=(anywhere,) * len(arrays),
        scratch_shapes=[pltpu.VMEM(a.shape, a.dtype) for a in arrays] + [sems, sems],
        compiler_params=pltpu.CompilerParams(vmem_limit_bytes=60 * 2**20),
        name="copy_out",
    )(*arrays)


def on_device(counts, cotangent, saved_gate, saved_up, down_weight):
    tok, ff = saved_gate.shape
    d = cotangent.shape[1]
    vmem = pl.BlockSpec(memory_space=pltpu.VMEM)
    anywhere = pl.BlockSpec(memory_space=pl.ANY)
    dma = pltpu.SemaphoreType.DMA
    results = pl.pallas_call(
        kernel,
        out_shape=(
            jax.ShapeDtypeStruct((tok, ff), jnp.bfloat16),
            jax.ShapeDtypeStruct((tok, ff), jnp.bfloat16),
            jax.ShapeDtypeStruct((ff, d), jnp.bfloat16),
        ),
        in_specs=[
            pl.BlockSpec(memory_space=pltpu.SMEM), anywhere, anywhere, anywhere, anywhere,
        ],
        out_specs=(vmem, vmem, anywhere),
        scratch_shapes=[
            pltpu.VMEM((tok, d), jnp.bfloat16),
            pltpu.VMEM((tok, ff), jnp.bfloat16),
            pltpu.VMEM((tok, ff), jnp.bfloat16),
            pltpu.VMEM((ff, d), jnp.bfloat16),
            pltpu.VMEM((GROUPS, tok, d), jnp.bfloat16),
            pltpu.VMEM((GROUPS, ff, tok), jnp.bfloat16),
            pltpu.VMEM((GROUPS, 2 * TILES, HALF, LANES), jnp.float32),
            pltpu.VMEM((2, HOPS, 2 * TILES, HALF, LANES), jnp.bfloat16),
            pltpu.VMEM((2, HOPS, 2 * TILES, HALF, LANES), jnp.bfloat16),
            pltpu.VMEM((2, TILES, tok, LANES), jnp.float32),
            pltpu.VMEM((ff, d), jnp.bfloat16),
            dma((4,)), dma, dma((8,)), dma((8,)), dma((8,)), dma((8,)),
            dma, dma((len(GATHER), 2, HOPS)), dma, dma((len(SCATTER), 2, HOPS)),
        ],
        compiler_params=pltpu.CompilerParams(
            collective_id=0, has_side_effects=True, vmem_limit_bytes=60 * 2**20
        ),
        cost_estimate=pl.CostEstimate(
            flops=4 * GROUPS * tok * ff * d, bytes_accessed=4 * ff * d + 8 * tok * ff, transcendentals=2 * tok * ff
        ),
        name="down_backward",
    )(counts, cotangent, saved_gate, saved_up, down_weight)
    return copied((1, 1, 2), *results)


def solution(mesh):
    return jax.shard_map(
        on_device,
        mesh=mesh,
        in_specs=(P(), P("col", "row"), P("row", "col"), P("row", "col"), P("col", "row")),
        out_specs=(P("row", "col"), P("row", "col"), P("col", "row")),
        check_vma=False,
    )
```

```python
import functools

import jax
import jax.numpy as jnp
from jax import lax
from jax.experimental import pallas as pl
from jax.experimental.pallas import tpu as pltpu
from jax.sharding import PartitionSpec as P

MESH = pl.DeviceIdType.MESH
GROUPS = 16
TOK = 128
LANES = 128
HOPS = 8
CUT = 32
CUTS = TOK // CUT


def streams(*rows):
    first, out = 0, []
    for kind, cut, longer, count in rows:
        out.append((kind, cut, longer, first, count))
        first += count
    return tuple(out)


GATHER = streams(
    ("zig", 0, 0, 6), ("zig", 1, 1, 6), ("loop", 0, 0, 3), ("loop", 2, 0, 3), ("loop", 4, 0, 3), ("loop", 6, 0, 3),
    ("zig", 0, 1, 8), ("zig", 1, 0, 8), ("loop", 1, 1, 3), ("loop", 3, 1, 3), ("loop", 5, 1, 3), ("loop", 7, 1, 3),
)
SCATTER = streams(
    ("zig", 0, 0, 6), ("zig", 1, 1, 6), ("loop", 0, 0, 3), ("loop", 2, 0, 3), ("loop", 4, 0, 3), ("loop", 6, 0, 3),
    ("zig", 0, 1, 8), ("zig", 1, 0, 8), ("loop", 1, 1, 3), ("loop", 3, 1, 3), ("loop", 5, 1, 3), ("loop", 7, 1, 3),
)
SETS = (range(0, 6), range(6, 12))
TILES = 13
SOURCES = ((0, 0), (1, 0), (0, 1), (0, 3), (0, 2), (1, 1), (1, 3), (1, 2))


def place(cycle, p):
    kind, cut = cycle[:2]
    p = lax.rem(p + 2 * GROUPS, GROUPS)
    if kind == "zig":
        z = p // 2
        x = lax.rem(p + z + cut, 2)
        return x * 8 + z
    x = p // 8
    z = x * (15 - p) + (1 - x) * p
    return x * 8 + lax.rem(z + cut + 1, 8)


def spot(cycle, row):
    kind, cut = cycle[:2]
    x = row // 8
    z = lax.rem(row, 8)
    if kind == "zig":
        return 2 * z + lax.rem(x + z + cut, 2)
    z = lax.rem(z + 15 - cut, 8)
    return x * (15 - z) + (1 - x) * z


def hops_of(cycle, d):
    return HOPS if d == cycle[2] else HOPS - 1


def kernel(
    counts_ref, cot_hbm, gate_hbm, up_hbm, weight_hbm,
    grad_gate_ref, grad_up_ref, grad_down_ref,
    cot_ref, gate_ref, up_ref, weight, cot, hid, part, stage, arrived, factors, down_out,
    load_sem, down_sem, cot_send, cot_recv, core_send, core_recv,
    hid_send, hid_recv, sum_send, sum_recv,
):
    row = lax.axis_index("row")
    col = lax.axis_index("col")
    x, z = row // 8, lax.rem(row, 8)
    xh = col // 8
    y = lax.rem(col // 2, 4)
    core = lax.rem(col, 2)

    def at_col(dx, dy, c):
        return lax.rem(xh + dx, 2) * 8 + lax.rem(y + dy, 4) * 2 + c

    pairs = ((cot_hbm, cot_ref), (gate_hbm, gate_ref), (up_hbm, up_ref), (weight_hbm, weight))
    loads = [pltpu.make_async_copy(*pair, load_sem.at[k]) for k, pair in enumerate(pairs)]
    for load in loads:
        load.start()

    barrier = pltpu.get_barrier_semaphore()
    rows = [(1 - x) * 8 + z, x * 8 + lax.rem(z + 1, 8), x * 8 + lax.rem(z + 7, 8)]
    cols = [at_col(0, 0, 1 - core)] + [at_col(dx, dy, core) for dx, dy in SOURCES[1:5]]
    for other in rows:
        pl.semaphore_signal(barrier, inc=1, device_id={"row": other}, device_id_type=MESH)
    for other in cols:
        pl.semaphore_signal(barrier, inc=1, device_id={"col": other}, device_id_type=MESH)

    limit = counts_ref[col]
    token = lax.broadcasted_iota(jnp.int32, cot_ref.shape, 0)
    loads[0].wait()
    cot[col] = jnp.where(token < limit, cot_ref[...], jnp.zeros_like(cot_ref))
    pl.semaphore_wait(barrier, len(rows) + len(cols))

    def cot_copy(q):
        dx, dy = SOURCES[q]
        block = cot.at[at_col(dx if dy else 0, 0, core)]
        target = at_col(0, 4 - dy, core) if dy else at_col(1, 0, core)
        return pltpu.make_async_remote_copy(
            src_ref=block, dst_ref=block, send_sem=cot_send.at[q], recv_sem=cot_recv.at[q],
            device_id={"col": target}, device_id_type=MESH,
        )

    def source(q):
        dx = jnp.where((q == 1) | (q > 4), 1, 0)
        dy = jnp.where((q == 2) | (q == 5), 1, 0) + jnp.where((q == 3) | (q == 6), 3, 0)
        dy = dy + jnp.where((q == 4) | (q == 7), 2, 0)
        return dx, dy

    def core_copy(q):
        dx, dy = source(q)
        block = cot.at[at_col(dx, dy, core)]
        return pltpu.make_async_remote_copy(
            src_ref=block, dst_ref=block, send_sem=core_send.at[q], recv_sem=core_recv.at[q],
            device_id={"col": at_col(0, 0, 1 - core)}, device_id_type=MESH,
        )

    def core_arrival(q):
        dx, dy = source(q)
        block = cot.at[at_col(dx, dy, 1 - core)]
        return pltpu.make_async_remote_copy(
            src_ref=block, dst_ref=block, send_sem=core_send.at[q], recv_sem=core_recv.at[q],
            device_id={"col": at_col(0, 0, 1 - core)}, device_id_type=MESH,
        )

    def cot_arrival(q):
        dx, dy = source(q)
        block = cot.at[at_col(dx, dy, core)]
        return pltpu.make_async_remote_copy(
            src_ref=block, dst_ref=block, send_sem=cot_send.at[q], recv_sem=cot_recv.at[q],
            device_id={"col": at_col(0, 0, 1 - core)}, device_id_type=MESH,
        )

    def hid_copy(i, d, s, shift=0):
        cycle = GATHER[i]
        p = spot(cycle, row)
        way = 1 - 2 * d
        block = hid.at[
            place(cycle, p - way * (s + shift)),
            pl.ds(cycle[3] * CUT, cycle[4] * CUT),
        ]
        return pltpu.make_async_remote_copy(
            src_ref=block, dst_ref=block, send_sem=hid_send, recv_sem=hid_recv.at[i, d, s],
            device_id={"row": place(cycle, p + way)}, device_id_type=MESH,
        )

    def sum_copy(i, d, s):
        cycle = SCATTER[i]
        tiles = pl.ds(cycle[3], cycle[4])
        return pltpu.make_async_remote_copy(
            src_ref=stage.at[d, s, tiles], dst_ref=arrived.at[d, s, tiles],
            send_sem=sum_send, recv_sem=sum_recv.at[i, d, s],
            device_id={"row": place(cycle, spot(cycle, row) + 1 - 2 * d)}, device_id_type=MESH,
        )

    def each(walks, s, run, picks=range(12)):
        for i in picks:
            cycle = walks[i]
            for d in range(2):
                if hops_of(cycle, d) < HOPS:
                    pl.when(s < HOPS - 1)(lambda i=i, d=d: run(i, d))
                else:
                    run(i, d)

    for q in range(1, 5):
        cot_copy(q).start()
    core_copy(0).start()

    loads[1].wait()
    loads[2].wait()
    tiles_done = 0
    for i, cycle in enumerate(GATHER):
        while CUTS * tiles_done < cycle[3] + cycle[4]:
            lanes = pl.ds(tiles_done * LANES, LANES)
            g = gate_ref[:, lanes].astype(jnp.float32)
            u = up_ref[:, lanes].astype(jnp.float32)
            hid[row, lanes, :] = (g * jax.nn.sigmoid(g) * u).T.astype(jnp.bfloat16)
            tiles_done += 1
        for d in range(2):
            hid_copy(i, d, 0).start()
    loads[3].wait()

    def pass_on(s, picks):
        def run(i, d):
            hid_copy(i, d, s - 1, 1).wait_recv()
            hid_copy(i, d, s).start()

        each(GATHER, s, run, picks)

    def partial_sums(q, carry):
        core_arrival(q).wait_recv()
        dx, dy = source(q)
        first = at_col(dx, dy, 0)
        block = cot[pl.ds(first, 2)].reshape(2 * TOK, cot.shape[2])
        for t in range(0, TILES, 2):
            n = min(2, TILES - t)
            product = lax.dot_general(
                block, weight[t * LANES:(t + n) * LANES, :], (((1,), (1,)), ((), ())),
                preferred_element_type=jnp.float32,
            )
            for k in range(n):
                piece = product[:, k * LANES:(k + 1) * LANES]
                part[pl.ds(first, 2), CUTS * (t + k):CUTS * (t + k + 1)] = piece.reshape(2, CUTS, CUT, LANES)
        return carry

    def across(q, carry):
        cot_arrival(q).wait_recv()
        core_copy(q).start()
        return carry

    def after(s):
        return lax.div(3 * s + 2, 2)

    def gather_step(s, carry):
        pass_on(s, SETS[0])

        @pl.when(s < 6)
        def _():
            lax.fori_loop(after(s - 1), after(s), across, 0)

        @pl.when(s == 1)
        def _():
            for q in range(5, 8):
                cot_copy(q).start()

        lax.fori_loop(jnp.where(s == 1, 0, after(s - 2)), after(s - 1), partial_sums, 0)
        pass_on(s, SETS[1])
        return carry

    lax.fori_loop(1, HOPS - 1, gather_step, 0)

    def sum_send_step(s, received, picks):
        def run(i, d):
            cycle = SCATTER[i]
            tiles = pl.ds(cycle[3], cycle[4])
            owner = place(cycle, spot(cycle, row) + (1 - 2 * d) * (hops_of(cycle, d) - s))
            value = part[owner, tiles]
            if received:
                sum_copy(i, d, s - 1).wait_recv()
                value = value + arrived[d, s - 1, tiles].astype(jnp.float32)
            stage[d, s, tiles] = value.astype(jnp.bfloat16)
            sum_copy(i, d, s).start()

        each(SCATTER, s, run, picks)

    for picks in SETS:
        sum_send_step(0, False, picks)
        pass_on(HOPS - 1, picks)

    def down(first, n):
        lhs = jnp.concatenate([hid[g, pl.ds(first, n), :] for g in range(GROUPS)], axis=1)
        down_out[pl.ds(first, n), :] = jnp.dot(
            lhs, cot[...].reshape(GROUPS * TOK, cot.shape[2]), preferred_element_type=jnp.float32
        ).astype(jnp.bfloat16)

    def down_piece(k, carry):
        down(pl.multiple_of(k * 2 * LANES, 2 * LANES), 2 * LANES)
        return carry

    def sum_step(s, carry):
        sum_send_step(s, True, SETS[0])

        @pl.when(s == 1)
        def _():
            for i, cycle in enumerate(GATHER):
                for d in range(2):
                    hid_copy(i, d, hops_of(cycle, d) - 1, 1).wait_recv()

        @pl.when(s > 1)
        def _():
            down_piece(s - 2, 0)

        sum_send_step(s, True, SETS[1])
        return carry

    lax.fori_loop(1, HOPS, sum_step, 0)
    down((TILES - 1) * LANES, LANES)

    store_down = pltpu.make_async_copy(down_out, grad_down_ref, down_sem)
    store_down.start()

    for t in range(TILES):
        lanes = pl.ds(t * LANES, LANES)
        g = gate_ref[:, lanes].astype(jnp.float32)
        u = up_ref[:, lanes].astype(jnp.float32)
        sig = jax.nn.sigmoid(g)
        factors[0, t] = g * sig
        factors[1, t] = u * (sig * (1.0 + g * (1.0 - sig)))

    for i, cycle in enumerate(SCATTER):
        tiles = pl.ds(cycle[3], cycle[4])
        total = part[row, tiles]
        for d in range(2):
            sum_copy(i, d, hops_of(cycle, d) - 1).wait_recv()
            total = total + arrived[d, hops_of(cycle, d) - 1, tiles].astype(jnp.float32)
        part[row, tiles] = total
    for t in range(TILES):
        lanes = pl.ds(t * LANES, LANES)
        grad = part[row, CUTS * t:CUTS * (t + 1)].reshape(TOK, LANES)
        up_ref[:, lanes] = (grad * factors[0, t]).astype(jnp.bfloat16)
        gate_ref[:, lanes] = (grad * factors[1, t]).astype(jnp.bfloat16)
    stores = [
        pltpu.make_async_copy(gate_ref, grad_gate_ref, load_sem.at[0]),
        pltpu.make_async_copy(up_ref, grad_up_ref, load_sem.at[1]),
    ]
    for store in stores:
        store.start()

    blocks = hid.at[pl.ds(0, GROUPS - 1)]
    for sem in (hid_send, sum_send):
        pltpu.make_async_copy(blocks, blocks, sem).wait()
    for q in range(8):
        core_copy(q).wait_send()
    for q in range(1, 8):
        cot_copy(q).wait_send()
    store_down.wait()
    for store in stores:
        store.wait()


def copy_kernel(pieces, *refs):
    n = len(refs) // 3
    take, give = refs[-2], refs[-1]
    steps, k = [], 0
    for a in range(n):
        source, target, held = refs[a], refs[n + a], refs[2 * n + a]
        rows = source.shape[0] // pieces[a]
        for p in range(pieces[a]):
            part = pl.ds(p * rows, rows)
            steps.append((
                pltpu.make_async_copy(source.at[part], held.at[part], take.at[k]),
                pltpu.make_async_copy(held.at[part], target.at[part], give.at[k]),
            ))
            k += 1
    for step in steps:
        step[0].start()
    for step in steps:
        step[0].wait()
        step[1].start()
    for step in steps:
        step[1].wait()


def copied(pieces, *arrays):
    anywhere = pl.BlockSpec(memory_space=pl.ANY)
    sems = pltpu.SemaphoreType.DMA((sum(pieces),))
    return pl.pallas_call(
        functools.partial(copy_kernel, pieces),
        out_shape=tuple(jax.ShapeDtypeStruct(a.shape, a.dtype) for a in arrays),
        in_specs=[anywhere] * len(arrays),
        out_specs=(anywhere,) * len(arrays),
        scratch_shapes=[pltpu.VMEM(a.shape, a.dtype) for a in arrays] + [sems, sems],
        compiler_params=pltpu.CompilerParams(vmem_limit_bytes=60 * 2**20),
        name="copy_out",
    )(*arrays)


def on_device(counts, cotangent, saved_gate, saved_up, down_weight):
    tok, ff = saved_gate.shape
    d = cotangent.shape[1]
    anywhere = pl.BlockSpec(memory_space=pl.ANY)
    dma = pltpu.SemaphoreType.DMA
    results = pl.pallas_call(
        kernel,
        out_shape=(
            jax.ShapeDtypeStruct((tok, ff), jnp.bfloat16),
            jax.ShapeDtypeStruct((tok, ff), jnp.bfloat16),
            jax.ShapeDtypeStruct((ff, d), jnp.bfloat16),
        ),
        in_specs=[
            pl.BlockSpec(memory_space=pltpu.SMEM), anywhere, anywhere, anywhere, anywhere,
        ],
        out_specs=(anywhere,) * 3,
        scratch_shapes=[
            pltpu.VMEM((tok, d), jnp.bfloat16),
            pltpu.VMEM((tok, ff), jnp.bfloat16),
            pltpu.VMEM((tok, ff), jnp.bfloat16),
            pltpu.VMEM((ff, d), jnp.bfloat16),
            pltpu.VMEM((GROUPS, tok, d), jnp.bfloat16),
            pltpu.VMEM((GROUPS, ff, tok), jnp.bfloat16),
            pltpu.VMEM((GROUPS, CUTS * TILES, CUT, LANES), jnp.float32),
            pltpu.VMEM((2, HOPS, CUTS * TILES, CUT, LANES), jnp.bfloat16),
            pltpu.VMEM((2, HOPS, CUTS * TILES, CUT, LANES), jnp.bfloat16),
            pltpu.VMEM((2, TILES, tok, LANES), jnp.float32),
            pltpu.VMEM((ff, d), jnp.bfloat16),
            dma((4,)), dma, dma((8,)), dma((8,)), dma((8,)), dma((8,)),
            dma, dma((len(GATHER), 2, HOPS)), dma, dma((len(SCATTER), 2, HOPS)),
        ],
        compiler_params=pltpu.CompilerParams(
            collective_id=0, has_side_effects=True, vmem_limit_bytes=60 * 2**20
        ),
        cost_estimate=pl.CostEstimate(
            flops=4 * GROUPS * tok * ff * d, bytes_accessed=4 * ff * d + 8 * tok * ff, transcendentals=2 * tok * ff
        ),
        name="down_backward",
    )(counts, cotangent, saved_gate, saved_up, down_weight)
    return copied((1, 1, 2), *results)


def solution(mesh):
    return jax.shard_map(
        on_device,
        mesh=mesh,
        in_specs=(P(), P("col", "row"), P("row", "col"), P("row", "col"), P("col", "row")),
        out_specs=(P("row", "col"), P("row", "col"), P("col", "row")),
        check_vma=False,
    )
```
